32 devices in a mesh: group: 2 (over y), src: 4 (over z), tgt: 2 (over x), prompt: 2 (over core).
Axes of the slice: x: 2, y: 2, z: 4, core: 2. Of those that a mesh axis runs over, the one named last changes fastest.
Arguments:
- decoder: bfloat16 [4, 2, 448, 4608], P('src', 'prompt'), may hold values from -6 to 6
- encoder: bfloat16 [2, 4, 64, 4608], P('prompt', 'src', None, 'tgt'), may hold values from -0.09375 to 0.09375
- activations: bfloat16 [64, 4, 448], P(('group', 'prompt'), 'src'), parts along dimension 0, may hold values from 0.0049743652 to 0.03491211
- prompt_mask: int32 [64, 4, 7], P(('group', 'prompt'), 'src'), parts along dimension 0, may hold values 0 or 1
- counts: int32 [8], P('group'), parts along dimension 0, may hold values from 1 to 6, as said below
Outputs:
- virtual: bfloat16 [8, 2, 4, 64, 448], P(('group', 'src'), 'prompt', None, 'tgt'), parts along dimension 0
- edges: float32 [64, 2, 4, 64], P(('group', 'prompt'), None, 'src', 'tgt'), parts along dimension 0
The draws below stay inside these ranges and needn't reach their ends.
There are 2 independent parts, one for each index of `group`. The reference program is written for one: setup_inputs(seed, part) draws one part's arguments, and reference() takes and returns one part's arrays. A program takes and returns all parts, laid end to end along the dimension named above; an argument that names none is the same for every part. Nothing has to cross between parts.
Inputs may be any that keep to these rules, and one draw needn't show every extreme that they name: counts[l] + counts[l + 2] == 7 for every l < 2.
All inputs are finite; a program needn't handle non-finite values. No bound on the sum of `prompt_mask` on one device may be relied on, other than what follows from the above.
Results may differ from the reference program's by a relative error of at most 0.0029.
Values may be sent and summed in bfloat16 or wider, within the bound.
No kernel may reach another device: no remote copies, remote signals or barrier semaphores. Data moves between devices by JAX's collectives and lax.ppermute only.
A program may use at most 64 MiB of HBM per device.

```python
import jax
import jax.numpy as jnp
from jax import lax

D = 4608
BLK = 64
TW = 64
SB = 7
SROWS = 448
L = 4
TL = 2
TBS = 4
PROMPTS = 32


def draw_counts(key, part):
    key = jax.random.fold_in(key, 7)
    half_layers = L // 2
    key_values = jax.random.fold_in(key, 1)
    key_place = jax.random.fold_in(key, 2)
    key_flip = jax.random.fold_in(key, 3)
    first_half = jax.random.randint(key_values, (half_layers,), 1, SB, dtype=jnp.int32)
    forced = jax.random.randint(key_place, (), 0, half_layers, dtype=jnp.int32)
    places = jnp.arange(half_layers, dtype=jnp.int32)
    first_half = jnp.where(places == forced, SB - 1, first_half).astype(jnp.int32)
    flips = jax.random.randint(key_flip, (half_layers,), 0, 2, dtype=jnp.int32)
    lower = jnp.where(flips == 1, SB - first_half, first_half).astype(jnp.int32)
    upper = (SB - lower).astype(jnp.int32)
    return jnp.concatenate([lower, upper]).astype(jnp.int32)


def set_ends(result, rng, least, high):
    index_at = [jax.random.randint(jax.random.fold_in(rng, axis), (), 0, length) for axis, length in enumerate(result.shape)]
    main_axis = result.shape.index(max(result.shape))
    neighbour = index_at[:main_axis] + [(index_at[main_axis] + 1) % result.shape[main_axis]] + index_at[main_axis + 1:]
    return result.at[tuple(index_at)].set(least).at[tuple(neighbour)].set(high)


def steps_of(stream_key, dims, shards, smallest, top_value):
    level = 1.0
    for dim, blocks in shards:
        draws = jax.random.uniform(jax.random.fold_in(jax.random.fold_in(stream_key, 6), dim), (blocks,), jnp.float32, smallest / len(shards), top_value / len(shards))
        level = level * jnp.repeat(jnp.exp(draws), dims[dim] // blocks).reshape((-1,) + (1,) * (len(dims) - 1 - dim))
    return level


def noise(rng, dims, width, reach, split=(), kind=jnp.bfloat16):
    drawn = jax.random.normal(rng, dims, jnp.float32) * width
    if len(split) > 0:
        drawn = steps_of(rng, dims, split, -0.22, 0.18) * drawn
    return jnp.clip(drawn, min=-reach, max=reach).astype(kind)


def setup_inputs(seed: int = 0, part: int = 0) -> dict:
    key_list = jax.random.split(jax.random.key(seed), 6)
    part_keys = jax.random.split(jax.random.fold_in(key_list[5], part), 6)
    decoder = noise(key_list[0], (L, TL, SROWS, D), 1.0, 6.0, ((0, 4), (1, 2)))
    encoder = noise(key_list[1], (TL, TBS, TW, D), D ** -0.5, 0.09375, ((0, 2), (1, 4), (3, 2)))
    activations = jnp.clip(0.0049743652 + 0.029937744 * jax.random.uniform(part_keys[2], (PROMPTS, L, SROWS), jnp.float32) ** steps_of(part_keys[2], (PROMPTS, L, SROWS), ((0, 2), (1, 4)), -0.2, 0.2), 0.0049743652, 0.03491211).astype(jnp.bfloat16)
    prompt_mask = set_ends((jax.random.randint(part_keys[3], (PROMPTS, L, SB), 0, 2) < 1).astype(jnp.int32), jax.random.fold_in(part_keys[3], 1), 0, 1)
    counts = draw_counts(jax.random.fold_in(jax.random.fold_in(key_list[5], part), 71), part)
    return dict(decoder=decoder, encoder=encoder, activations=activations, prompt_mask=prompt_mask, counts=counts)


def reference(decoder, encoder, activations, prompt_mask, counts):
    block_ids = jnp.arange(SROWS, dtype=jnp.int32) // BLK
    live_rows = (block_ids[None, :] < counts[:, None]).astype(jnp.float32)
    encoder_wide = encoder.astype(jnp.float32)

    def one_layer(inputs):
        layer_decoder, layer_live = inputs
        products = jnp.einsum("tkwd,trd->tkwr", encoder_wide, layer_decoder.astype(jnp.float32))
        return (products * layer_live).astype(jnp.bfloat16)

    virtual = lax.map(one_layer, (decoder, live_rows))
    mask_rows = jnp.repeat(prompt_mask, BLK, axis=2).astype(jnp.float32)
    weights = (activations.astype(jnp.float32) * mask_rows * live_rows[None, :, :]).astype(jnp.bfloat16)

    def add_layer(total, inputs):
        layer_weights, layer_virtual = inputs
        term = jnp.einsum("pr,tkwr->ptkw", layer_weights.astype(jnp.float32), layer_virtual.astype(jnp.float32))
        return total + term, 0

    start_total = jnp.zeros((PROMPTS, TL, TBS, TW), jnp.float32)
    edges, unused = lax.scan(add_layer, start_total, (jnp.swapaxes(weights, 0, 1), virtual))
    return virtual, edges
```

```python
import jax
import jax.numpy as jnp
from jax import lax
from jax.sharding import PartitionSpec as P

AXES = ("group", "src", "tgt")


def own_weights(activations, prompt_mask, blocks_live, rows):
    slots = rows * prompt_mask.shape[2] // activations.shape[2]
    block = activations.shape[2] // prompt_mask.shape[2]
    mask = prompt_mask[:, 0, :slots] * blocks_live[None, :slots].astype(jnp.int32)
    return activations[:, 0, :rows] * jnp.repeat(mask, block, axis=1).astype(activations.dtype)


def any_mesh(decoder, encoder, activations, prompt_mask, counts):
    row_count, slot_count = decoder.shape[2], prompt_mask.shape[2]
    blocks_live = jnp.arange(slot_count, dtype=jnp.int32) < counts[lax.axis_index("src")]
    weights = own_weights(activations, prompt_mask, blocks_live, row_count)
    part = lax.all_to_all(encoder, "tgt", split_axis=2, concat_axis=3, tiled=True)
    blocks = lax.all_gather(part, "src", axis=1, tiled=True)[0]
    products = jnp.einsum("kwd,rd->kwr", blocks, decoder[0, 0], preferred_element_type=jnp.float32)
    virtual = jnp.where(jnp.repeat(blocks_live, row_count // slot_count), products, 0.0).astype(jnp.bfloat16)
    both = lax.all_gather(weights, "prompt", axis=0, tiled=True)
    terms = jnp.einsum("pr,kwr->pkw", both, virtual, preferred_element_type=jnp.float32)
    terms = lax.psum_scatter(terms, "src", scatter_dimension=1, tiled=True)
    edges = lax.all_to_all(terms[:, None], "prompt", split_axis=0, concat_axis=1, tiled=True)
    return virtual[None, None], edges


def square_mesh(decoder, encoder, activations, prompt_mask, counts):
    row_count, slot_count = decoder.shape[2], prompt_mask.shape[2]
    block_rows = row_count // slot_count
    rows = row_count - block_rows
    y, z, x, core = (lax.axis_index(a) for a in ("group", "src", "tgt", "prompt"))
    features, width = encoder.shape[2] // 2, encoder.shape[3]

    def place(y, z, x):
        return (y * 4 + z) * 2 + x

    def swapped(pairs):
        return [(place(y, a, x), place(x, b, y)) for y in range(2) for x in range(2) for a, b in pairs]

    def step(s):
        return [(i, i ^ s) for i in range(4)]

    piece = lax.dynamic_slice_in_dim(encoder[0, 0], y * features, features, axis=0)
    far = lax.ppermute(piece, AXES, swapped(step(2)))
    near = lax.ppermute(piece, AXES, swapped(step(1)))
    own = lax.ppermute(piece, AXES, swapped(step(0)))
    last = lax.ppermute(far, "src", step(1))

    blocks_live = jnp.arange(slot_count, dtype=jnp.int32) < counts[z]
    live = jnp.repeat(blocks_live, block_rows)[:rows]
    mine = own_weights(activations, prompt_mask, blocks_live, rows)
    other = lax.ppermute(mine, "prompt", [(0, 1), (1, 0)])
    weights = jnp.concatenate([mine, other])

    slab = lax.dynamic_slice(decoder[0, 0], (0, y * width), (rows, width))

    def products(blocks):
        return jnp.einsum("kwd,rd->kwr", blocks, slab, preferred_element_type=jnp.float32)

    def finish(part):
        total = part + lax.ppermute(part, "group", [(0, 1), (1, 0)])
        return jnp.where(live, total, 0.0).astype(jnp.bfloat16)

    def terms(virtual):
        return jnp.einsum("pr,kwr->kpw", weights, virtual, preferred_element_type=jnp.float32)

    first = finish(products(jnp.stack([own, near, far])))
    first_terms = terms(first)
    final = finish(products(last[None]))
    final_terms = terms(final)
    total = first_terms[0] + lax.ppermute(first_terms[1], "src", step(1)) + lax.ppermute(first_terms[2], "src", step(2))
    total = total + lax.ppermute(final_terms[0], "src", step(3))
    half = total.shape[0] // 2
    theirs = lax.ppermute(total[half:], "prompt", [(0, 1), (1, 0)])
    keep = total[:half]
    edges = jnp.where(core == 0, jnp.stack([keep, theirs], 1), jnp.stack([theirs, keep], 1))
    held = jnp.concatenate([first, final])
    virtual = jnp.stack([lax.dynamic_index_in_dim(held, jnp.bitwise_xor(z, k), 0, keepdims=False) for k in range(4)])
    virtual = jnp.pad(virtual, ((0, 0), (0, 0), (0, row_count - rows)))
    return virtual[None, None], edges[:, :, None]


def solution(mesh):
    placed = (
        P("src", "prompt", None, None),
        P("prompt", "src", None, "tgt"),
        P(("group", "prompt"), "src", None),
        P(("group", "prompt"), "src", None),
        P("group"),
    )
    square = mesh.shape["group"] == 2 and mesh.shape["tgt"] == 2 and mesh.shape["src"] == 4
    return jax.shard_map(
        square_mesh if square else any_mesh,
        mesh=mesh,
        in_specs=placed,
        out_specs=(
            P(("group", "src"), "prompt", None, "tgt", None),
            P(("group", "prompt"), None, "src", "tgt"),
        ),
        check_vma=False,
    )
```

```python
import jax
import jax.numpy as jnp
from jax import lax
from jax.experimental import pallas as pl
from jax.experimental.pallas import tpu as pltpu
from jax.sharding import PartitionSpec as P

AXES = ("group", "src", "tgt")


def own_weights(activations, prompt_mask, blocks_live, rows):
    slots = rows * prompt_mask.shape[2] // activations.shape[2]
    block = activations.shape[2] // prompt_mask.shape[2]
    mask = prompt_mask[:, 0, :slots] * blocks_live[None, :slots].astype(jnp.int32)
    return activations[:, 0, :rows] * jnp.repeat(mask, block, axis=1).astype(activations.dtype)


def mask_kernel(counts_ref, activations_ref, mask_ref, weights_ref, live_ref):
    slots, rows = mask_ref.shape[0], weights_ref.shape[1]
    block = activations_ref.shape[1] // slots
    row_slot = lax.broadcasted_iota(jnp.int32, (slots, rows), 1) // block
    in_slot = row_slot == lax.broadcasted_iota(jnp.int32, (slots, rows), 0)
    spread = jnp.where(in_slot & (row_slot < counts_ref[lax.axis_index("src")]), 1.0, 0.0)
    mask = mask_ref[...].reshape(slots, mask_ref.shape[2]).astype(jnp.float32)
    spread_mask = lax.dot_general(mask, spread, (((0,), (0,)), ((), ())), preferred_element_type=jnp.float32)
    weights_ref[...] = (activations_ref[:, :rows].astype(jnp.float32) * spread_mask).astype(weights_ref.dtype)
    live_ref[...] = jnp.broadcast_to(jnp.sum(spread, axis=0, keepdims=True), live_ref.shape)


def masked(counts, activations, prompt_mask, rows):
    whole = pl.BlockSpec(memory_space=pltpu.VMEM)
    return pl.pallas_call(
        mask_kernel,
        out_shape=(
            jax.ShapeDtypeStruct((activations.shape[0], rows), activations.dtype),
            jax.ShapeDtypeStruct((8, rows), jnp.float32),
        ),
        in_specs=[pl.BlockSpec(memory_space=pltpu.SMEM), whole, whole],
        out_specs=(whole, whole),
    )(counts, activations[:, 0], jnp.transpose(prompt_mask, (2, 1, 0)))


def any_mesh(decoder, encoder, activations, prompt_mask, counts):
    row_count, slot_count = decoder.shape[2], prompt_mask.shape[2]
    blocks_live = jnp.arange(slot_count, dtype=jnp.int32) < counts[lax.axis_index("src")]
    weights = own_weights(activations, prompt_mask, blocks_live, row_count)
    part = lax.all_to_all(encoder, "tgt", split_axis=2, concat_axis=3, tiled=True)
    blocks = lax.all_gather(part, "src", axis=1, tiled=True)[0]
    products = jnp.einsum("kwd,rd->kwr", blocks, decoder[0, 0], preferred_element_type=jnp.float32)
    virtual = jnp.where(jnp.repeat(blocks_live, row_count // slot_count), products, 0.0).astype(jnp.bfloat16)
    both = lax.all_gather(weights, "prompt", axis=0, tiled=True)
    terms = jnp.einsum("pr,kwr->pkw", both, virtual, preferred_element_type=jnp.float32)
    terms = lax.psum_scatter(terms, "src", scatter_dimension=1, tiled=True)
    edges = lax.all_to_all(terms[:, None], "prompt", split_axis=0, concat_axis=1, tiled=True)
    return virtual[None, None], edges


def square_mesh(decoder, encoder, activations, prompt_mask, counts):
    row_count, slot_count = decoder.shape[2], prompt_mask.shape[2]
    block_rows = row_count // slot_count
    rows = row_count - block_rows
    y, z, x, core = (lax.axis_index(a) for a in ("group", "src", "tgt", "prompt"))
    features, width = encoder.shape[2] // 2, encoder.shape[3]

    def place(y, z, x):
        return (y * 4 + z) * 2 + x

    def swapped(pairs):
        return [(place(y, a, x), place(x, b, y)) for y in range(2) for x in range(2) for a, b in pairs]

    def step(s):
        return [(i, i ^ s) for i in range(4)]

    swap = [(0, 1), (1, 0)]
    piece = lax.optimization_barrier(lax.dynamic_slice_in_dim(encoder[0, 0], y * features, features, axis=0))
    beside = lax.dynamic_slice_in_dim(encoder[0, 0], (1 - y) * features, features, axis=0)
    far = lax.ppermute(piece, AXES, swapped(step(2)))
    near = lax.ppermute(piece, AXES, swapped(step(1)))
    given = lax.ppermute(beside, ("group", "tgt"), [(0, 1), (3, 2)])
    last = lax.ppermute(far, "src", step(1))
    own = jnp.where(x == y, piece, given)
    slab = lax.optimization_barrier(lax.dynamic_slice(decoder[0, 0], (0, y * width), (rows, width)))
    mine, live = masked(counts, activations, prompt_mask, rows)
    weights = jnp.concatenate([mine, lax.ppermute(mine, "prompt", swap)])

    def products(blocks):
        return jnp.einsum("kwd,rd->kwr", blocks, slab, preferred_element_type=jnp.float32)

    def finish(part):
        total = part + lax.ppermute(part, "group", swap)
        return jnp.where(live[0] > 0, total, 0.0).astype(jnp.bfloat16)

    def terms(virtual):
        return jnp.einsum("pr,kwr->kpw", weights, virtual, preferred_element_type=jnp.float32)

    first = finish(products(jnp.stack([own, near, far])))
    first_terms = terms(first)
    final = finish(products(last[None]))
    final_terms = terms(final)
    total = first_terms[0] + lax.ppermute(first_terms[1], "src", step(1)) + lax.ppermute(first_terms[2], "src", step(2))
    total = total + lax.ppermute(final_terms[0], "src", step(3))
    half = total.shape[0] // 2
    theirs = lax.ppermute(total[half:], "prompt", swap)
    keep = total[:half]
    edges = jnp.where(core == 0, jnp.stack([keep, theirs], 1), jnp.stack([theirs, keep], 1))
    held = jnp.concatenate([first, final])
    virtual = jnp.stack([lax.dynamic_index_in_dim(held, jnp.bitwise_xor(z, k), 0, keepdims=False) for k in range(4)])
    virtual = jnp.pad(virtual, ((0, 0), (0, 0), (0, row_count - rows)))
    return virtual[None, None], edges[:, :, None]


def solution(mesh):
    placed = (
        P("src", "prompt", None, None),
        P("prompt", "src", None, "tgt"),
        P(("group", "prompt"), "src", None),
        P(("group", "prompt"), "src", None),
        P("group"),
    )
    square = mesh.shape["group"] == 2 and mesh.shape["tgt"] == 2 and mesh.shape["src"] == 4
    return jax.shard_map(
        square_mesh if square else any_mesh,
        mesh=mesh,
        in_specs=placed,
        out_specs=(
            P(("group", "src"), "prompt", None, "tgt", None),
            P(("group", "prompt"), None, "src", "tgt"),
        ),
        check_vma=False,
    )
```

```python
import jax
import jax.numpy as jnp
from jax import lax
from jax.experimental import pallas as pl
from jax.experimental.pallas import tpu as pltpu
from jax.sharding import PartitionSpec as P

AXES = ("group", "src", "tgt")


def own_weights(activations, prompt_mask, blocks_live, rows):
    slots = rows * prompt_mask.shape[2] // activations.shape[2]
    block = activations.shape[2] // prompt_mask.shape[2]
    mask = prompt_mask[:, 0, :slots] * blocks_live[None, :slots].astype(jnp.int32)
    return activations[:, 0, :rows] * jnp.repeat(mask, block, axis=1).astype(activations.dtype)


def mask_kernel(counts_ref, activations_ref, mask_ref, weights_ref, live_ref):
    slots, rows = mask_ref.shape[0], weights_ref.shape[1]
    block = activations_ref.shape[1] // slots
    row_slot = lax.broadcasted_iota(jnp.int32, (slots, rows), 1) // block
    in_slot = row_slot == lax.broadcasted_iota(jnp.int32, (slots, rows), 0)
    spread = jnp.where(in_slot & (row_slot < counts_ref[lax.axis_index("src")]), 1.0, 0.0)
    mask = mask_ref[...].reshape(slots, mask_ref.shape[2]).astype(jnp.float32)
    spread_mask = lax.dot_general(mask, spread, (((0,), (0,)), ((), ())), preferred_element_type=jnp.float32)
    weights_ref[...] = (activations_ref[:, :rows].astype(jnp.float32) * spread_mask).astype(weights_ref.dtype)
    live_ref[...] = jnp.broadcast_to(jnp.sum(spread, axis=0, keepdims=True), live_ref.shape)


def masked(counts, activations, prompt_mask, rows):
    whole = pl.BlockSpec(memory_space=pltpu.VMEM)
    return pl.pallas_call(
        mask_kernel,
        out_shape=(
            jax.ShapeDtypeStruct((activations.shape[0], rows), activations.dtype),
            jax.ShapeDtypeStruct((8, rows), jnp.float32),
        ),
        in_specs=[pl.BlockSpec(memory_space=pltpu.SMEM), whole, whole],
        out_specs=(whole, whole),
    )(counts, activations[:, 0], jnp.transpose(prompt_mask, (2, 1, 0)))


def any_mesh(decoder, encoder, activations, prompt_mask, counts):
    row_count, slot_count = decoder.shape[2], prompt_mask.shape[2]
    blocks_live = jnp.arange(slot_count, dtype=jnp.int32) < counts[lax.axis_index("src")]
    weights = own_weights(activations, prompt_mask, blocks_live, row_count)
    part = lax.all_to_all(encoder, "tgt", split_axis=2, concat_axis=3, tiled=True)
    blocks = lax.all_gather(part, "src", axis=1, tiled=True)[0]
    products = jnp.einsum("kwd,rd->kwr", blocks, decoder[0, 0], preferred_element_type=jnp.float32)
    virtual = jnp.where(jnp.repeat(blocks_live, row_count // slot_count), products, 0.0).astype(jnp.bfloat16)
    both = lax.all_gather(weights, "prompt", axis=0, tiled=True)
    terms = jnp.einsum("pr,kwr->pkw", both, virtual, preferred_element_type=jnp.float32)
    terms = lax.psum_scatter(terms, "src", scatter_dimension=1, tiled=True)
    edges = lax.all_to_all(terms[:, None], "prompt", split_axis=0, concat_axis=1, tiled=True)
    return virtual[None, None], edges


def square_mesh(decoder, encoder, activations, prompt_mask, counts):
    row_count, slot_count = decoder.shape[2], prompt_mask.shape[2]
    block_rows = row_count // slot_count
    rows = row_count - block_rows
    y, z, x, core = (lax.axis_index(a) for a in ("group", "src", "tgt", "prompt"))
    features, width = encoder.shape[2] // 2, encoder.shape[3]

    def place(y, z, x):
        return (y * 4 + z) * 2 + x

    def swapped(pairs):
        return [(place(y, a, x), place(x, b, y)) for y in range(2) for x in range(2) for a, b in pairs]

    def step(s):
        return [(i, i ^ s) for i in range(4)]

    swap = [(0, 1), (1, 0)]
    piece = lax.optimization_barrier(lax.dynamic_slice_in_dim(encoder[0, 0], y * features, features, axis=0))
    far = lax.ppermute(piece, AXES, swapped(step(3)))
    near = lax.ppermute(piece, AXES, swapped(step(1)))
    last = lax.ppermute(far, "src", step(1))
    slab = lax.optimization_barrier(lax.dynamic_slice(decoder[0, 0], (0, y * width), (rows, width)))

    def products(blocks):
        return jnp.einsum("kwd,rd->kwr", blocks, slab, preferred_element_type=jnp.float32)

    def finish(part, narrow, after=None):
        if narrow:
            sent = lax.ppermute((part * 16).astype(jnp.float16), "group", swap)
            if after is not None:
                sent, _ = lax.optimization_barrier((sent, after))
            total = part + sent.astype(jnp.float32) * 0.0625
        else:
            sent = lax.ppermute(part, "group", swap)
            if after is not None:
                sent, _ = lax.optimization_barrier((sent, after))
            total = part + sent
        return jnp.where(live[0] > 0, total, 0.0).astype(jnp.bfloat16)

    def terms(virtual):
        return jnp.einsum("pr,kwr->kpw", weights, virtual, preferred_element_type=jnp.float32)

    whole = encoder[0, 0].reshape(2, features, width)
    halves = products(whole)
    counts, _ = lax.optimization_barrier((counts, halves))
    mine, live = masked(counts, activations, prompt_mask, rows)
    weights = jnp.concatenate([mine, lax.ppermute(mine, "prompt", swap)])
    across = lax.ppermute(jnp.where(x == 0, halves[1], halves[0]), "tgt", swap)
    own = jnp.where(x == y, jnp.where(x == 0, halves[0], halves[1]), across)
    early = jnp.concatenate([own[None], products(jnp.stack([near, far]))])
    first = finish(early, False, last)
    first_terms = terms(first)
    final = finish(products(last[None]), False)
    final_terms = terms(final)
    total = first_terms[0] + lax.ppermute(first_terms[1], "src", step(1)) + lax.ppermute(first_terms[2], "src", step(3))
    total = total + lax.ppermute(final_terms[0], "src", step(2))
    held = jnp.stack([first[0], first[1], final[0], first[2]])
    half = total.shape[0] // 2
    theirs = lax.ppermute(total[half:], "prompt", swap)
    keep = total[:half]
    edges = jnp.where(core == 0, jnp.stack([keep, theirs], 1), jnp.stack([theirs, keep], 1))
    virtual = jnp.stack([lax.dynamic_index_in_dim(held, jnp.bitwise_xor(z, k), 0, keepdims=False) for k in range(4)])
    virtual = jnp.pad(virtual, ((0, 0), (0, 0), (0, row_count - rows)))
    return virtual[None, None], edges[:, :, None]


def solution(mesh):
    placed = (
        P("src", "prompt", None, None),
        P("prompt", "src", None, "tgt"),
        P(("group", "prompt"), "src", None),
        P(("group", "prompt"), "src", None),
        P("group"),
    )
    square = mesh.shape["group"] == 2 and mesh.shape["tgt"] == 2 and mesh.shape["src"] == 4
    return jax.shard_map(
        square_mesh if square else any_mesh,
        mesh=mesh,
        in_specs=placed,
        out_specs=(
            P(("group", "src"), "prompt", None, "tgt", None),
            P(("group", "prompt"), None, "src", "tgt"),
        ),
        check_vma=False,
    )
```

```python
import jax
import jax.numpy as jnp
from jax import lax
from jax.experimental import pallas as pl
from jax.experimental.pallas import tpu as pltpu
from jax.sharding import PartitionSpec as P

AXES = ("group", "src", "tgt")


def own_weights(activations, prompt_mask, blocks_live, rows):
    slots = rows * prompt_mask.shape[2] // activations.shape[2]
    block = activations.shape[2] // prompt_mask.shape[2]
    mask = prompt_mask[:, 0, :slots] * blocks_live[None, :slots].astype(jnp.int32)
    return activations[:, 0, :rows] * jnp.repeat(mask, block, axis=1).astype(activations.dtype)


def mask_kernel(counts_ref, activations_ref, mask_ref, weights_ref, live_ref):
    slots, rows = mask_ref.shape[0], weights_ref.shape[1]
    block = activations_ref.shape[1] // slots
    row_slot = lax.broadcasted_iota(jnp.int32, (slots, rows), 1) // block
    in_slot = row_slot == lax.broadcasted_iota(jnp.int32, (slots, rows), 0)
    spread = jnp.where(in_slot & (row_slot < counts_ref[lax.axis_index("src")]), 1.0, 0.0)
    mask = mask_ref[...].reshape(slots, mask_ref.shape[2]).astype(jnp.float32)
    spread_mask = lax.dot_general(mask, spread, (((0,), (0,)), ((), ())), preferred_element_type=jnp.float32)
    weights_ref[...] = (activations_ref[:, :rows].astype(jnp.float32) * spread_mask).astype(weights_ref.dtype)
    live_ref[...] = jnp.broadcast_to(jnp.sum(spread, axis=0, keepdims=True), live_ref.shape)


def masked(counts, activations, prompt_mask, rows):
    whole = pl.BlockSpec(memory_space=pltpu.VMEM)
    return pl.pallas_call(
        mask_kernel,
        out_shape=(
            jax.ShapeDtypeStruct((activations.shape[0], rows), activations.dtype),
            jax.ShapeDtypeStruct((8, rows), jnp.float32),
        ),
        in_specs=[pl.BlockSpec(memory_space=pltpu.SMEM), whole, whole],
        out_specs=(whole, whole),
    )(counts, activations[:, 0], jnp.transpose(prompt_mask, (2, 1, 0)))


def any_mesh(decoder, encoder, activations, prompt_mask, counts):
    row_count, slot_count = decoder.shape[2], prompt_mask.shape[2]
    blocks_live = jnp.arange(slot_count, dtype=jnp.int32) < counts[lax.axis_index("src")]
    weights = own_weights(activations, prompt_mask, blocks_live, row_count)
    part = lax.all_to_all(encoder, "tgt", split_axis=2, concat_axis=3, tiled=True)
    blocks = lax.all_gather(part, "src", axis=1, tiled=True)[0]
    products = jnp.einsum("kwd,rd->kwr", blocks, decoder[0, 0], preferred_element_type=jnp.float32)
    virtual = jnp.where(jnp.repeat(blocks_live, row_count // slot_count), products, 0.0).astype(jnp.bfloat16)
    both = lax.all_gather(weights, "prompt", axis=0, tiled=True)
    terms = jnp.einsum("pr,kwr->pkw", both, virtual, preferred_element_type=jnp.float32)
    terms = lax.psum_scatter(terms, "src", scatter_dimension=1, tiled=True)
    edges = lax.all_to_all(terms[:, None], "prompt", split_axis=0, concat_axis=1, tiled=True)
    return virtual[None, None], edges


def square_mesh(decoder, encoder, activations, prompt_mask, counts):
    row_count, slot_count = decoder.shape[2], prompt_mask.shape[2]
    block_rows = row_count // slot_count
    rows = row_count - block_rows
    y, z, x, core = (lax.axis_index(a) for a in ("group", "src", "tgt", "prompt"))
    features, width = encoder.shape[2] // 2, encoder.shape[3]

    def place(y, z, x):
        return (y * 4 + z) * 2 + x

    def swapped(pairs):
        return [(place(y, a, x), place(x, b, y)) for y in range(2) for x in range(2) for a, b in pairs]

    def step(s):
        return [(i, i ^ s) for i in range(4)]

    swap = [(0, 1), (1, 0)]
    piece = lax.optimization_barrier(lax.dynamic_slice_in_dim(encoder[0, 0], y * features, features, axis=0))
    far = lax.ppermute(piece, AXES, swapped(step(3)))
    near = lax.ppermute(piece, AXES, swapped(step(1)))
    last = lax.ppermute(far, "src", step(1))
    slab = lax.optimization_barrier(lax.dynamic_slice(decoder[0, 0], (0, y * width), (rows, width)))
    mine, live = masked(counts, activations, prompt_mask, rows)
    weights = jnp.concatenate([mine, lax.ppermute(mine, "prompt", swap)])

    def products(blocks, slab):
        return jnp.einsum("kwd,rd->kwr", blocks, slab, preferred_element_type=jnp.float32)

    def swapped_sum(part, sent, axis, narrow, after=None):
        if narrow:
            sent = (sent * 16).astype(jnp.float16)
        sent = lax.ppermute(sent, axis, swap)
        if after is not None:
            sent, _ = lax.optimization_barrier((sent, after))
        if narrow:
            sent = sent.astype(jnp.float32) * 0.0625
        return jnp.where(live[0] > 0, part + sent, 0.0).astype(jnp.bfloat16)

    def terms(virtual):
        return jnp.einsum("pr,kwr->kpw", weights, virtual, preferred_element_type=jnp.float32)

    whole = encoder[0, 0].reshape(2, features, width)
    own_slab = lax.optimization_barrier(lax.dynamic_slice(decoder[0, 0], (0, x * width), (rows, width)))
    halves = products(whole, own_slab)
    ours, theirs = jnp.where(x == 0, halves, halves[::-1])
    early = products(jnp.stack([near, far]), slab)
    ours, theirs, _ = lax.optimization_barrier((ours, theirs, early))
    own = swapped_sum(ours[None], theirs[None], "tgt", False)
    early = swapped_sum(early, early, "group", False, last)
    near_terms, far_terms = terms(early)
    late = products(last[None], slab)
    late = swapped_sum(late, late, "group", False)
    last_terms = terms(late)[0]
    total = terms(own)[0] + lax.ppermute(near_terms, "src", step(1)) + lax.ppermute(far_terms, "src", step(3))
    total = total + lax.ppermute(last_terms, "src", step(2))
    half = total.shape[0] // 2
    theirs = lax.ppermute(total[half:], "prompt", swap)
    keep = total[:half]
    edges = jnp.where(core == 0, jnp.stack([keep, theirs], 1), jnp.stack([theirs, keep], 1))
    held = jnp.stack([own[0], early[0], late[0], early[1]])
    virtual = jnp.stack([lax.dynamic_index_in_dim(held, jnp.bitwise_xor(z, k), 0, keepdims=False) for k in range(4)])
    virtual = jnp.pad(virtual, ((0, 0), (0, 0), (0, row_count - rows)))
    return virtual[None, None], edges[:, :, None]


def solution(mesh):
    placed = (
        P("src", "prompt", None, None),
        P("prompt", "src", None, "tgt"),
        P(("group", "prompt"), "src", None),
        P(("group", "prompt"), "src", None),
        P("group"),
    )
    square = mesh.shape["group"] == 2 and mesh.shape["tgt"] == 2 and mesh.shape["src"] == 4
    return jax.shard_map(
        square_mesh if square else any_mesh,
        mesh=mesh,
        in_specs=placed,
        out_specs=(
            P(("group", "src"), "prompt", None, "tgt", None),
            P(("group", "prompt"), None, "src", "tgt"),
        ),
        check_vma=False,
    )
```

```python
import jax
import jax.numpy as jnp
from jax import lax
from jax.experimental import pallas as pl
from jax.experimental.pallas import tpu as pltpu
from jax.sharding import PartitionSpec as P

AXES = ("group", "src", "tgt")


def own_weights(activations, prompt_mask, blocks_live, rows):
    slots = rows * prompt_mask.shape[2] // activations.shape[2]
    block = activations.shape[2] // prompt_mask.shape[2]
    mask = prompt_mask[:, 0, :slots] * blocks_live[None, :slots].astype(jnp.int32)
    return activations[:, 0, :rows] * jnp.repeat(mask, block, axis=1).astype(activations.dtype)


def mask_kernel(counts_ref, activations_ref, mask_ref, weights_ref, live_ref):
    slots, rows = mask_ref.shape[0], weights_ref.shape[1]
    block = activations_ref.shape[1] // slots
    row_slot = lax.broadcasted_iota(jnp.int32, (slots, rows), 1) // block
    in_slot = row_slot == lax.broadcasted_iota(jnp.int32, (slots, rows), 0)
    spread = jnp.where(in_slot & (row_slot < counts_ref[lax.axis_index("src")]), 1.0, 0.0)
    mask = mask_ref[...].reshape(slots, mask_ref.shape[2]).astype(jnp.float32)
    spread_mask = lax.dot_general(mask, spread, (((0,), (0,)), ((), ())), preferred_element_type=jnp.float32)
    weights_ref[...] = (activations_ref[:, :rows].astype(jnp.float32) * spread_mask).astype(weights_ref.dtype)
    live_ref[...] = jnp.broadcast_to(jnp.sum(spread, axis=0, keepdims=True), live_ref.shape)


def masked(counts, activations, prompt_mask, rows):
    whole = pl.BlockSpec(memory_space=pltpu.VMEM)
    return pl.pallas_call(
        mask_kernel,
        out_shape=(
            jax.ShapeDtypeStruct((activations.shape[0], rows), activations.dtype),
            jax.ShapeDtypeStruct((8, rows), jnp.float32),
        ),
        in_specs=[pl.BlockSpec(memory_space=pltpu.SMEM), whole, whole],
        out_specs=(whole, whole),
    )(counts, activations[:, 0], jnp.transpose(prompt_mask, (2, 1, 0)))


def any_mesh(decoder, encoder, activations, prompt_mask, counts):
    row_count, slot_count = decoder.shape[2], prompt_mask.shape[2]
    blocks_live = jnp.arange(slot_count, dtype=jnp.int32) < counts[lax.axis_index("src")]
    weights = own_weights(activations, prompt_mask, blocks_live, row_count)
    part = lax.all_to_all(encoder, "tgt", split_axis=2, concat_axis=3, tiled=True)
    blocks = lax.all_gather(part, "src", axis=1, tiled=True)[0]
    products = jnp.einsum("kwd,rd->kwr", blocks, decoder[0, 0], preferred_element_type=jnp.float32)
    virtual = jnp.where(jnp.repeat(blocks_live, row_count // slot_count), products, 0.0).astype(jnp.bfloat16)
    both = lax.all_gather(weights, "prompt", axis=0, tiled=True)
    terms = jnp.einsum("pr,kwr->pkw", both, virtual, preferred_element_type=jnp.float32)
    terms = lax.psum_scatter(terms, "src", scatter_dimension=1, tiled=True)
    edges = lax.all_to_all(terms[:, None], "prompt", split_axis=0, concat_axis=1, tiled=True)
    return virtual[None, None], edges


def square_mesh(decoder, encoder, activations, prompt_mask, counts):
    row_count, slot_count = decoder.shape[2], prompt_mask.shape[2]
    block_rows = row_count // slot_count
    rows = row_count - block_rows
    y, z, x, core = (lax.axis_index(a) for a in ("group", "src", "tgt", "prompt"))
    features, width = encoder.shape[2] // 2, encoder.shape[3]

    def place(y, z, x):
        return (y * 4 + z) * 2 + x

    def swapped(pairs):
        return [(place(y, a, x), place(x, b, y)) for y in range(2) for x in range(2) for a, b in pairs]

    def step(s):
        return [(i, i ^ s) for i in range(4)]

    swap = [(0, 1), (1, 0)]
    piece = lax.optimization_barrier(lax.dynamic_slice_in_dim(encoder[0, 0], y * features, features, axis=0))
    far = lax.ppermute(piece, AXES, swapped(step(3)))
    near = lax.ppermute(piece, AXES, swapped(step(1)))
    last = lax.ppermute(far, "src", step(1))
    slab = lax.optimization_barrier(lax.dynamic_slice(decoder[0, 0], (0, y * width), (rows, width)))
    mine, live = masked(counts, activations, prompt_mask, rows)
    weights = jnp.concatenate([mine, lax.ppermute(mine, "prompt", swap)])

    def products(blocks, slab):
        return jnp.einsum("kwd,rd->kwr", blocks, slab, preferred_element_type=jnp.float32)

    def swapped_sum(part, sent, axis, narrow, after=None):
        if narrow:
            sent = (sent * 16).astype(jnp.float16)
        sent = lax.ppermute(sent, axis, swap)
        if after is not None:
            sent, _ = lax.optimization_barrier((sent, after))
        if narrow:
            sent = sent.astype(jnp.float32) * 0.0625
        return jnp.where(live[0] > 0, part + sent, 0.0).astype(jnp.bfloat16)

    def terms(virtual):
        return jnp.einsum("pr,kwr->kpw", weights, virtual, preferred_element_type=jnp.float32)

    whole = encoder[0, 0].reshape(2, features, width)
    own_slab = lax.optimization_barrier(lax.dynamic_slice(decoder[0, 0], (0, x * width), (rows, width)))
    halves = products(whole, own_slab)
    ours, theirs = jnp.where(x == 0, halves, halves[::-1])
    early = products(jnp.stack([near, far]), slab)
    ours, theirs, _ = lax.optimization_barrier((ours, theirs, early))
    own = swapped_sum(ours[None], theirs[None], "tgt", False)
    early = swapped_sum(early, early, "group", False, last)
    near_terms, far_terms = terms(early)
    late = products(last[None], slab)
    late = swapped_sum(late, late, "group", False)
    last_terms = terms(late)[0]
    total = terms(own)[0] + lax.ppermute(far_terms, "src", step(3)) + lax.ppermute(near_terms, "src", step(1))
    total = total + lax.ppermute(last_terms, "src", step(2))
    half = total.shape[0] // 2
    theirs = lax.ppermute(total[half:], "prompt", swap)
    keep = total[:half]
    edges = jnp.where(core == 0, jnp.stack([keep, theirs], 1), jnp.stack([theirs, keep], 1))
    held = jnp.stack([own[0], early[0], late[0], early[1]])
    virtual = jnp.stack([lax.dynamic_index_in_dim(held, jnp.bitwise_xor(z, k), 0, keepdims=False) for k in range(4)])
    virtual = jnp.pad(virtual, ((0, 0), (0, 0), (0, row_count - rows)))
    return virtual[None, None], edges[:, :, None]


def solution(mesh):
    placed = (
        P("src", "prompt", None, None),
        P("prompt", "src", None, "tgt"),
        P(("group", "prompt"), "src", None),
        P(("group", "prompt"), "src", None),
        P("group"),
    )
    square = mesh.shape["group"] == 2 and mesh.shape["tgt"] == 2 and mesh.shape["src"] == 4
    return jax.shard_map(
        square_mesh if square else any_mesh,
        mesh=mesh,
        in_specs=placed,
        out_specs=(
            P(("group", "src"), "prompt", None, "tgt", None),
            P(("group", "prompt"), None, "src", "tgt"),
        ),
        check_vma=False,
    )
```

```python
import jax
import jax.numpy as jnp
from jax import lax
from jax.experimental import pallas as pl
from jax.experimental.pallas import tpu as pltpu
from jax.sharding import PartitionSpec as P

AXES = ("group", "src", "tgt")


def own_weights(activations, prompt_mask, blocks_live, rows):
    slots = rows * prompt_mask.shape[2] // activations.shape[2]
    block = activations.shape[2] // prompt_mask.shape[2]
    mask = prompt_mask[:, 0, :slots] * blocks_live[None, :slots].astype(jnp.int32)
    return activations[:, 0, :rows] * jnp.repeat(mask, block, axis=1).astype(activations.dtype)


def mask_kernel(counts_ref, activations_ref, mask_ref, weights_ref, live_ref):
    slots, rows = mask_ref.shape[0], weights_ref.shape[1]
    block = activations_ref.shape[1] // slots
    row_slot = lax.broadcasted_iota(jnp.int32, (slots, rows), 1) // block
    in_slot = row_slot == lax.broadcasted_iota(jnp.int32, (slots, rows), 0)
    spread = jnp.where(in_slot & (row_slot < counts_ref[lax.axis_index("src")]), 1.0, 0.0)
    mask = mask_ref[...].reshape(slots, mask_ref.shape[2]).astype(jnp.float32)
    spread_mask = lax.dot_general(mask, spread, (((0,), (0,)), ((), ())), preferred_element_type=jnp.float32)
    weights_ref[...] = (activations_ref[:, :rows].astype(jnp.float32) * spread_mask).astype(weights_ref.dtype)
    live_ref[...] = jnp.broadcast_to(jnp.sum(spread, axis=0, keepdims=True), live_ref.shape)


def masked(counts, activations, prompt_mask, rows):
    whole = pl.BlockSpec(memory_space=pltpu.VMEM)
    return pl.pallas_call(
        mask_kernel,
        out_shape=(
            jax.ShapeDtypeStruct((activations.shape[0], rows), activations.dtype),
            jax.ShapeDtypeStruct((8, rows), jnp.float32),
        ),
        in_specs=[pl.BlockSpec(memory_space=pltpu.SMEM), whole, whole],
        out_specs=(whole, whole),
    )(counts, activations[:, 0], jnp.transpose(prompt_mask, (2, 1, 0)))


def any_mesh(decoder, encoder, activations, prompt_mask, counts):
    row_count, slot_count = decoder.shape[2], prompt_mask.shape[2]
    blocks_live = jnp.arange(slot_count, dtype=jnp.int32) < counts[lax.axis_index("src")]
    weights = own_weights(activations, prompt_mask, blocks_live, row_count)
    part = lax.all_to_all(encoder, "tgt", split_axis=2, concat_axis=3, tiled=True)
    blocks = lax.all_gather(part, "src", axis=1, tiled=True)[0]
    products = jnp.einsum("kwd,rd->kwr", blocks, decoder[0, 0], preferred_element_type=jnp.float32)
    virtual = jnp.where(jnp.repeat(blocks_live, row_count // slot_count), products, 0.0).astype(jnp.bfloat16)
    both = lax.all_gather(weights, "prompt", axis=0, tiled=True)
    terms = jnp.einsum("pr,kwr->pkw", both, virtual, preferred_element_type=jnp.float32)
    terms = lax.psum_scatter(terms, "src", scatter_dimension=1, tiled=True)
    edges = lax.all_to_all(terms[:, None], "prompt", split_axis=0, concat_axis=1, tiled=True)
    return virtual[None, None], edges


def square_mesh(decoder, encoder, activations, prompt_mask, counts):
    row_count, slot_count = decoder.shape[2], prompt_mask.shape[2]
    block_rows = row_count // slot_count
    rows = row_count - block_rows
    y, z, x, core = (lax.axis_index(a) for a in ("group", "src", "tgt", "prompt"))
    features, width = encoder.shape[2] // 2, encoder.shape[3]

    def place(y, z, x):
        return (y * 4 + z) * 2 + x

    def swapped(pairs):
        return [(place(y, a, x), place(x, b, y)) for y in range(2) for x in range(2) for a, b in pairs]

    def step(s):
        return [(i, i ^ s) for i in range(4)]

    swap = [(0, 1), (1, 0)]
    piece = lax.optimization_barrier(lax.dynamic_slice_in_dim(encoder[0, 0], y * features, features, axis=0))
    far = lax.ppermute(piece, AXES, swapped(step(3)))
    near = lax.ppermute(piece, AXES, swapped(step(1)))
    last = lax.ppermute(far, "src", step(1))
    slab = lax.optimization_barrier(lax.dynamic_slice(decoder[0, 0], (0, y * width), (rows, width)))
    mine, live = masked(counts, activations, prompt_mask, rows)
    weights = jnp.concatenate([mine, lax.ppermute(mine, "prompt", swap)])

    def products(blocks, slab):
        return jnp.einsum("kwd,rd->kwr", blocks, slab, preferred_element_type=jnp.float32)

    def swapped_sum(part, sent, axis, after=None):
        sent = lax.ppermute(sent, axis, swap)
        if after is not None:
            sent, _ = lax.optimization_barrier((sent, after))
        return jnp.where(live[0] > 0, part + sent, 0.0).astype(jnp.bfloat16)

    def terms(virtual):
        return jnp.einsum("pr,kwr->kpw", weights, virtual, preferred_element_type=jnp.float32)

    whole = encoder[0, 0].reshape(2, features, width)
    own_slab = lax.optimization_barrier(lax.dynamic_slice(decoder[0, 0], (0, x * width), (rows, width)))
    halves = products(whole, own_slab)
    ours, theirs = jnp.where(x == 0, halves, halves[::-1])
    early = products(jnp.stack([near, far]), slab)
    ours, theirs, _ = lax.optimization_barrier((ours, theirs, early))
    own = swapped_sum(ours[None], theirs[None], "tgt")
    early = swapped_sum(early, early, "group", after=last)
    near_terms, far_terms = terms(early)
    late = products(last[None], slab)
    late = swapped_sum(late, late, "group")
    last_terms = terms(late)[0]
    total = terms(own)[0] + lax.ppermute(far_terms, "src", step(3)) + lax.ppermute(near_terms, "src", step(1))
    total = total + lax.ppermute(last_terms, "src", step(2))
    half = total.shape[0] // 2
    theirs = lax.ppermute(total[half:], "prompt", swap)
    keep = total[:half]
    edges = jnp.where(core == 0, jnp.stack([keep, theirs], 1), jnp.stack([theirs, keep], 1))
    held = jnp.stack([own[0], early[0], late[0], early[1]])
    virtual = jnp.stack([lax.dynamic_index_in_dim(held, jnp.bitwise_xor(z, k), 0, keepdims=False) for k in range(4)])
    virtual = jnp.pad(virtual, ((0, 0), (0, 0), (0, row_count - rows)))
    return virtual[None, None], edges[:, :, None]


def solution(mesh):
    placed = (
        P("src", "prompt", None, None),
        P("prompt", "src", None, "tgt"),
        P(("group", "prompt"), "src", None),
        P(("group", "prompt"), "src", None),
        P("group"),
    )
    square = mesh.shape["group"] == 2 and mesh.shape["tgt"] == 2 and mesh.shape["src"] == 4
    return jax.shard_map(
        square_mesh if square else any_mesh,
        mesh=mesh,
        in_specs=placed,
        out_specs=(
            P(("group", "src"), "prompt", None, "tgt", None),
            P(("group", "prompt"), None, "src", "tgt"),
        ),
        check_vma=False,
    )
```

```python
import jax
import jax.numpy as jnp
from jax import lax
from jax.experimental import pallas as pl
from jax.experimental.pallas import tpu as pltpu
from jax.sharding import PartitionSpec as P

AXES = ("group", "src", "tgt")


def own_weights(activations, prompt_mask, blocks_live, rows):
    slots = rows * prompt_mask.shape[2] // activations.shape[2]
    block = activations.shape[2] // prompt_mask.shape[2]
    mask = prompt_mask[:, 0, :slots] * blocks_live[None, :slots].astype(jnp.int32)
    return activations[:, 0, :rows] * jnp.repeat(mask, block, axis=1).astype(activations.dtype)


def mask_kernel(counts_ref, activations_ref, mask_ref, weights_ref, live_ref):
    slots, rows = mask_ref.shape[0], weights_ref.shape[1]
    block = activations_ref.shape[1] // slots
    row_slot = lax.broadcasted_iota(jnp.int32, (slots, rows), 1) // block
    in_slot = row_slot == lax.broadcasted_iota(jnp.int32, (slots, rows), 0)
    spread = jnp.where(in_slot & (row_slot < counts_ref[lax.axis_index("src")]), 1.0, 0.0)
    mask = mask_ref[...].reshape(slots, mask_ref.shape[2]).astype(jnp.float32)
    spread_mask = lax.dot_general(mask, spread, (((0,), (0,)), ((), ())), preferred_element_type=jnp.float32)
    weights_ref[...] = (activations_ref[:, :rows].astype(jnp.float32) * spread_mask).astype(weights_ref.dtype)
    live_ref[...] = jnp.broadcast_to(jnp.sum(spread, axis=0, keepdims=True), live_ref.shape)


def masked(counts, activations, prompt_mask, rows):
    whole = pl.BlockSpec(memory_space=pltpu.VMEM)
    return pl.pallas_call(
        mask_kernel,
        out_shape=(
            jax.ShapeDtypeStruct((activations.shape[0], rows), activations.dtype),
            jax.ShapeDtypeStruct((8, rows), jnp.float32),
        ),
        in_specs=[pl.BlockSpec(memory_space=pltpu.SMEM), whole, whole],
        out_specs=(whole, whole),
    )(counts, activations[:, 0], jnp.transpose(prompt_mask, (2, 1, 0)))


def any_mesh(decoder, encoder, activations, prompt_mask, counts):
    row_count, slot_count = decoder.shape[2], prompt_mask.shape[2]
    blocks_live = jnp.arange(slot_count, dtype=jnp.int32) < counts[lax.axis_index("src")]
    weights = own_weights(activations, prompt_mask, blocks_live, row_count)
    part = lax.all_to_all(encoder, "tgt", split_axis=2, concat_axis=3, tiled=True)
    blocks = lax.all_gather(part, "src", axis=1, tiled=True)[0]
    products = jnp.einsum("kwd,rd->kwr", blocks, decoder[0, 0], preferred_element_type=jnp.float32)
    virtual = jnp.where(jnp.repeat(blocks_live, row_count // slot_count), products, 0.0).astype(jnp.bfloat16)
    both = lax.all_gather(weights, "prompt", axis=0, tiled=True)
    terms = jnp.einsum("pr,kwr->pkw", both, virtual, preferred_element_type=jnp.float32)
    terms = lax.psum_scatter(terms, "src", scatter_dimension=1, tiled=True)
    edges = lax.all_to_all(terms[:, None], "prompt", split_axis=0, concat_axis=1, tiled=True)
    return virtual[None, None], edges


def square_mesh(decoder, encoder, activations, prompt_mask, counts):
    row_count, slot_count = decoder.shape[2], prompt_mask.shape[2]
    block_rows = row_count // slot_count
    rows = row_count - block_rows
    y, z, x, core = (lax.axis_index(a) for a in ("group", "src", "tgt", "prompt"))
    features, width = encoder.shape[2] // 2, encoder.shape[3]

    def place(y, z, x):
        return (y * 4 + z) * 2 + x

    def swapped(pairs):
        return [(place(y, a, x), place(x, b, y)) for y in range(2) for x in range(2) for a, b in pairs]

    def step(s):
        return [(i, i ^ s) for i in range(4)]

    swap = [(0, 1), (1, 0)]
    piece = lax.optimization_barrier(lax.dynamic_slice_in_dim(encoder[0, 0], y * features, features, axis=0))
    far = lax.ppermute(piece, AXES, swapped(step(3)))
    near = lax.ppermute(piece, AXES, swapped(step(1)))
    last = lax.ppermute(far, "src", step(1))
    slab = lax.optimization_barrier(lax.dynamic_slice(decoder[0, 0], (0, y * width), (rows, width)))
    mine, live = masked(counts, activations, prompt_mask, rows)
    weights = jnp.stack([mine, lax.ppermute(mine, "prompt", swap)])

    def products(blocks, slab):
        return jnp.einsum("kwd,rd->kwr", blocks, slab, preferred_element_type=jnp.float32)

    def swapped_sum(part, sent, axis, after=None):
        sent = lax.ppermute(sent, axis, swap)
        if after is not None:
            sent, _ = lax.optimization_barrier((sent, after))
        return jnp.where(live[0] > 0, part + sent, 0.0).astype(jnp.bfloat16)

    def terms(virtual):
        out = jnp.einsum("spr,kwr->kspw", weights, virtual, preferred_element_type=jnp.float32)
        return out.reshape(out.shape[0], -1, features)

    whole = encoder[0, 0].reshape(2, features, width)
    own_slab = lax.optimization_barrier(lax.dynamic_slice(decoder[0, 0], (0, x * width), (rows, width)))
    halves = products(whole, own_slab)
    ours, theirs = jnp.where(x == 0, halves, halves[::-1])
    early = jnp.concatenate([products(near[None], slab), products(far[None], slab)])
    ours, theirs, _ = lax.optimization_barrier((ours, theirs, early))
    own = swapped_sum(ours[None], theirs[None], "tgt")
    early = swapped_sum(early, early, "group", after=last)
    near_terms, far_terms = terms(early)
    late = products(last[None], slab)
    late = swapped_sum(late, late, "group")
    last_terms = terms(late)[0]
    total = terms(own)[0] + lax.ppermute(far_terms, "src", step(3)) + lax.ppermute(near_terms, "src", step(1))
    total = total + lax.ppermute(last_terms, "src", step(2))
    half = total.shape[0] // 2
    theirs = lax.ppermute(total[half:], "prompt", swap)
    keep = total[:half]
    edges = jnp.where(core == 0, jnp.stack([keep, theirs], 1), jnp.stack([theirs, keep], 1))
    held = jnp.stack([own[0], early[0], late[0], early[1]])
    virtual = jnp.stack([lax.dynamic_index_in_dim(held, jnp.bitwise_xor(z, k), 0, keepdims=False) for k in range(4)])
    virtual = jnp.pad(virtual, ((0, 0), (0, 0), (0, row_count - rows)))
    return virtual[None, None], edges[:, :, None]


def solution(mesh):
    placed = (
        P("src", "prompt", None, None),
        P("prompt", "src", None, "tgt"),
        P(("group", "prompt"), "src", None),
        P(("group", "prompt"), "src", None),
        P("group"),
    )
    square = mesh.shape["group"] == 2 and mesh.shape["tgt"] == 2 and mesh.shape["src"] == 4
    return jax.shard_map(
        square_mesh if square else any_mesh,
        mesh=mesh,
        in_specs=placed,
        out_specs=(
            P(("group", "src"), "prompt", None, "tgt", None),
            P(("group", "prompt"), None, "src", "tgt"),
        ),
        check_vma=False,
    )
```

```python
import jax
import jax.numpy as jnp
from jax import lax
from jax.experimental import pallas as pl
from jax.experimental.pallas import tpu as pltpu
from jax.sharding import PartitionSpec as P

AXES = ("group", "src", "tgt")


def own_weights(activations, prompt_mask, blocks_live, rows):
    slots = rows * prompt_mask.shape[2] // activations.shape[2]
    block = activations.shape[2] // prompt_mask.shape[2]
    mask = prompt_mask[:, 0, :slots] * blocks_live[None, :slots].astype(jnp.int32)
    return activations[:, 0, :rows] * jnp.repeat(mask, block, axis=1).astype(activations.dtype)


def mask_kernel(counts_ref, activations_ref, mask_ref, weights_ref, live_ref):
    slots, rows = mask_ref.shape[0], weights_ref.shape[1]
    block = activations_ref.shape[1] // slots
    row_slot = lax.broadcasted_iota(jnp.int32, (slots, rows), 1) // block
    in_slot = row_slot == lax.broadcasted_iota(jnp.int32, (slots, rows), 0)
    spread = jnp.where(in_slot & (row_slot < counts_ref[lax.axis_index("src")]), 1.0, 0.0)
    mask = mask_ref[...].reshape(slots, mask_ref.shape[2]).astype(jnp.float32)
    spread_mask = lax.dot_general(mask, spread, (((0,), (0,)), ((), ())), preferred_element_type=jnp.float32)
    weights_ref[...] = (activations_ref[:, :rows].astype(jnp.float32) * spread_mask).astype(weights_ref.dtype)
    live_ref[...] = jnp.broadcast_to(jnp.sum(spread, axis=0, keepdims=True), live_ref.shape)


def masked(counts, activations, prompt_mask, rows):
    whole = pl.BlockSpec(memory_space=pltpu.VMEM)
    return pl.pallas_call(
        mask_kernel,
        out_shape=(
            jax.ShapeDtypeStruct((activations.shape[0], rows), activations.dtype),
            jax.ShapeDtypeStruct((8, rows), jnp.float32),
        ),
        in_specs=[pl.BlockSpec(memory_space=pltpu.SMEM), whole, whole],
        out_specs=(whole, whole),
    )(counts, activations[:, 0], jnp.transpose(prompt_mask, (2, 1, 0)))


def any_mesh(decoder, encoder, activations, prompt_mask, counts):
    row_count, slot_count = decoder.shape[2], prompt_mask.shape[2]
    blocks_live = jnp.arange(slot_count, dtype=jnp.int32) < counts[lax.axis_index("src")]
    weights = own_weights(activations, prompt_mask, blocks_live, row_count)
    part = lax.all_to_all(encoder, "tgt", split_axis=2, concat_axis=3, tiled=True)
    blocks = lax.all_gather(part, "src", axis=1, tiled=True)[0]
    products = jnp.einsum("kwd,rd->kwr", blocks, decoder[0, 0], preferred_element_type=jnp.float32)
    virtual = jnp.where(jnp.repeat(blocks_live, row_count // slot_count), products, 0.0).astype(jnp.bfloat16)
    both = lax.all_gather(weights, "prompt", axis=0, tiled=True)
    terms = jnp.einsum("pr,kwr->pkw", both, virtual, preferred_element_type=jnp.float32)
    terms = lax.psum_scatter(terms, "src", scatter_dimension=1, tiled=True)
    edges = lax.all_to_all(terms[:, None], "prompt", split_axis=0, concat_axis=1, tiled=True)
    return virtual[None, None], edges


def square_mesh(decoder, encoder, activations, prompt_mask, counts):
    row_count, slot_count = decoder.shape[2], prompt_mask.shape[2]
    block_rows = row_count // slot_count
    rows = row_count - block_rows
    y, z, x, core = (lax.axis_index(a) for a in ("group", "src", "tgt", "prompt"))
    features, width = encoder.shape[2] // 2, encoder.shape[3]

    def place(y, z, x):
        return (y * 4 + z) * 2 + x

    def swapped(pairs):
        return [(place(y, a, x), place(x, b, y)) for y in range(2) for x in range(2) for a, b in pairs]

    def step(s):
        return [(i, i ^ s) for i in range(4)]

    swap = [(0, 1), (1, 0)]
    piece = lax.optimization_barrier(lax.dynamic_slice_in_dim(encoder[0, 0], y * features, features, axis=0))
    far = lax.ppermute(piece, AXES, swapped(step(3)))
    near = lax.ppermute(piece, AXES, swapped(step(1)))
    last = lax.ppermute(far, "src", step(1))
    slab = lax.optimization_barrier(lax.dynamic_slice(decoder[0, 0], (0, y * width), (rows, width)))
    mine, live = masked(counts, activations, prompt_mask, rows)
    weights = jnp.stack([mine, lax.ppermute(mine, "prompt", swap)])

    def products(blocks, slab):
        return jnp.einsum("kwd,rd->kwr", blocks, slab, preferred_element_type=jnp.float32)

    def swapped_sum(part, sent, axis, after=None):
        sent = lax.ppermute(sent, axis, swap)
        if after is not None:
            sent, _ = lax.optimization_barrier((sent, after))
        return ((part + sent) * live[0]).astype(jnp.bfloat16)

    def terms(virtual):
        out = jnp.einsum("spr,kwr->kspw", weights, virtual, preferred_element_type=jnp.float32)
        return out.reshape(out.shape[0], -1, features)

    whole = encoder[0, 0].reshape(2, features, width)
    own_slab = lax.optimization_barrier(lax.dynamic_slice(decoder[0, 0], (0, x * width), (rows, width)))
    halves = products(whole, own_slab)
    ours, theirs = jnp.where(x == 0, halves, halves[::-1])
    early = products(jnp.stack([near, far]), slab)
    ours, theirs, _ = lax.optimization_barrier((ours, theirs, early))
    own = swapped_sum(ours[None], theirs[None], "tgt")
    early = swapped_sum(early, early, "group", after=last)
    near_terms, far_terms = terms(early)
    late = products(last[None], slab)
    late = swapped_sum(late, late, "group")
    last_terms = terms(late)[0]
    total = terms(own)[0] + lax.ppermute(far_terms, "src", step(3)) + lax.ppermute(near_terms, "src", step(1))
    total = total + lax.ppermute(last_terms, "src", step(2))
    half = total.shape[0] // 2
    theirs = lax.ppermute(total[half:], "prompt", swap)
    keep = total[:half]
    edges = jnp.where(core == 0, jnp.stack([keep, theirs], 1), jnp.stack([theirs, keep], 1))
    held = jnp.stack([own[0], early[0], late[0], early[1]])
    virtual = jnp.stack([lax.dynamic_index_in_dim(held, jnp.bitwise_xor(z, k), 0, keepdims=False) for k in range(4)])
    virtual = jnp.pad(virtual, ((0, 0), (0, 0), (0, row_count - rows)))
    return virtual[None, None], edges[:, :, None]


def solution(mesh):
    placed = (
        P("src", "prompt", None, None),
        P("prompt", "src", None, "tgt"),
        P(("group", "prompt"), "src", None),
        P(("group", "prompt"), "src", None),
        P("group"),
    )
    square = mesh.shape["group"] == 2 and mesh.shape["tgt"] == 2 and mesh.shape["src"] == 4
    return jax.shard_map(
        square_mesh if square else any_mesh,
        mesh=mesh,
        in_specs=placed,
        out_specs=(
            P(("group", "src"), "prompt", None, "tgt", None),
            P(("group", "prompt"), None, "src", "tgt"),
        ),
        check_vma=False,
    )
```

```python
import jax
import jax.numpy as jnp
from jax import lax
from jax.experimental import pallas as pl
from jax.experimental.pallas import tpu as pltpu
from jax.sharding import PartitionSpec as P

AXES = ("group", "src", "tgt")


def own_weights(activations, prompt_mask, blocks_live, rows):
    slots = rows * prompt_mask.shape[2] // activations.shape[2]
    block = activations.shape[2] // prompt_mask.shape[2]
    mask = prompt_mask[:, 0, :slots] * blocks_live[None, :slots].astype(jnp.int32)
    return activations[:, 0, :rows] * jnp.repeat(mask, block, axis=1).astype(activations.dtype)


def mask_kernel(counts_ref, activations_ref, mask_ref, weights_ref, live_ref):
    slots, rows = mask_ref.shape[0], weights_ref.shape[1]
    block = activations_ref.shape[1] // slots
    row_slot = lax.broadcasted_iota(jnp.int32, (slots, rows), 1) // block
    in_slot = row_slot == lax.broadcasted_iota(jnp.int32, (slots, rows), 0)
    spread = jnp.where(in_slot & (row_slot < counts_ref[lax.axis_index("src")]), 1.0, 0.0)
    mask = mask_ref[...].reshape(slots, mask_ref.shape[2]).astype(jnp.float32)
    spread_mask = lax.dot_general(mask, spread, (((0,), (0,)), ((), ())), preferred_element_type=jnp.float32)
    weights_ref[...] = (activations_ref[:, :rows].astype(jnp.float32) * spread_mask).astype(weights_ref.dtype)
    live_ref[...] = jnp.broadcast_to(jnp.sum(spread, axis=0, keepdims=True), live_ref.shape)


def masked(counts, activations, prompt_mask, rows):
    whole = pl.BlockSpec(memory_space=pltpu.VMEM)
    return pl.pallas_call(
        mask_kernel,
        out_shape=(
            jax.ShapeDtypeStruct((activations.shape[0], rows), activations.dtype),
            jax.ShapeDtypeStruct((8, rows), jnp.float32),
        ),
        in_specs=[pl.BlockSpec(memory_space=pltpu.SMEM), whole, whole],
        out_specs=(whole, whole),
    )(counts, activations[:, 0], jnp.transpose(prompt_mask, (2, 1, 0)))


def any_mesh(decoder, encoder, activations, prompt_mask, counts):
    row_count, slot_count = decoder.shape[2], prompt_mask.shape[2]
    blocks_live = jnp.arange(slot_count, dtype=jnp.int32) < counts[lax.axis_index("src")]
    weights = own_weights(activations, prompt_mask, blocks_live, row_count)
    part = lax.all_to_all(encoder, "tgt", split_axis=2, concat_axis=3, tiled=True)
    blocks = lax.all_gather(part, "src", axis=1, tiled=True)[0]
    products = jnp.einsum("kwd,rd->kwr", blocks, decoder[0, 0], preferred_element_type=jnp.float32)
    virtual = jnp.where(jnp.repeat(blocks_live, row_count // slot_count), products, 0.0).astype(jnp.bfloat16)
    both = lax.all_gather(weights, "prompt", axis=0, tiled=True)
    terms = jnp.einsum("pr,kwr->pkw", both, virtual, preferred_element_type=jnp.float32)
    terms = lax.psum_scatter(terms, "src", scatter_dimension=1, tiled=True)
    edges = lax.all_to_all(terms[:, None], "prompt", split_axis=0, concat_axis=1, tiled=True)
    return virtual[None, None], edges


def square_mesh(decoder, encoder, activations, prompt_mask, counts):
    row_count, slot_count = decoder.shape[2], prompt_mask.shape[2]
    block_rows = row_count // slot_count
    rows = row_count - block_rows
    y, z, x, core = (lax.axis_index(a) for a in ("group", "src", "tgt", "prompt"))
    features, width = encoder.shape[2] // 2, encoder.shape[3]

    def place(y, z, x):
        return (y * 4 + z) * 2 + x

    def swapped(pairs):
        return [(place(y, a, x), place(x, b, y)) for y in range(2) for x in range(2) for a, b in pairs]

    def step(s):
        return [(i, i ^ s) for i in range(4)]

    swap = [(0, 1), (1, 0)]
    piece = lax.optimization_barrier(lax.dynamic_slice_in_dim(encoder[0, 0], y * features, features, axis=0))
    far = lax.ppermute(piece, AXES, swapped(step(3)))
    near = lax.ppermute(piece, AXES, swapped(step(1)))
    last = lax.ppermute(far, "src", step(1))
    slab = lax.optimization_barrier(lax.dynamic_slice(decoder[0, 0], (0, y * width), (rows, width)))
    mine, live = masked(counts, activations, prompt_mask, rows)
    weights = jnp.stack([mine, lax.ppermute(mine, "prompt", swap)])

    def products(blocks, slab):
        return jnp.einsum("kwd,rd->kwr", blocks, slab, preferred_element_type=jnp.float32)

    def swapped_sum(part, sent, axis, after=None):
        sent = lax.ppermute(sent, axis, swap)
        if after is not None:
            sent, _ = lax.optimization_barrier((sent, after))
        return ((part + sent) * live[0]).astype(jnp.bfloat16)

    def terms(virtual):
        out = jnp.einsum("spr,kwr->kspw", weights, virtual, preferred_element_type=jnp.float32)
        return out.reshape(out.shape[0], -1, features)

    whole = encoder[0, 0].reshape(2, features, width)
    own_slab = lax.optimization_barrier(lax.dynamic_slice(decoder[0, 0], (0, x * width), (rows, width)))
    halves = products(whole, own_slab)
    ours, theirs = jnp.where(x == 0, halves, halves[::-1])
    early = products(jnp.stack([near, far]), slab)
    ours, theirs, _ = lax.optimization_barrier((ours, theirs, early))
    own = swapped_sum(ours[None], theirs[None], "tgt")
    early = swapped_sum(early, early, "group", after=last)
    near_terms, far_terms = terms(early)
    late = products(last[None], slab)
    late = swapped_sum(late, late, "group")
    last_terms = terms(late)[0]
    total = lax.ppermute(far_terms, "src", step(3)) + lax.ppermute(near_terms, "src", step(1)) + terms(own)[0]
    total = total + lax.ppermute(last_terms, "src", step(2))
    half = total.shape[0] // 2
    theirs = lax.ppermute(total[half:], "prompt", swap)
    keep = total[:half]
    edges = jnp.where(core == 0, jnp.stack([keep, theirs], 1), jnp.stack([theirs, keep], 1))
    held = jnp.stack([own[0], early[0], late[0], early[1]])
    virtual = jnp.stack([lax.dynamic_index_in_dim(held, jnp.bitwise_xor(z, k), 0, keepdims=False) for k in range(4)])
    virtual = jnp.pad(virtual, ((0, 0), (0, 0), (0, row_count - rows)))
    return virtual[None, None], edges[:, :, None]


def solution(mesh):
    placed = (
        P("src", "prompt", None, None),
        P("prompt", "src", None, "tgt"),
        P(("group", "prompt"), "src", None),
        P(("group", "prompt"), "src", None),
        P("group"),
    )
    square = mesh.shape["group"] == 2 and mesh.shape["tgt"] == 2 and mesh.shape["src"] == 4
    return jax.shard_map(
        square_mesh if square else any_mesh,
        mesh=mesh,
        in_specs=placed,
        out_specs=(
            P(("group", "src"), "prompt", None, "tgt", None),
            P(("group", "prompt"), None, "src", "tgt"),
        ),
        check_vma=False,
    )
```
